32 devices in a mesh: grain: 4 (over z), row: 8 (over y, x, core).
Axes of the slice: x: 2, y: 2, z: 4, core: 2. Of those that a mesh axis runs over, the one named last changes fastest.
Arguments:
- order_params: float32 [64, 4, 1024, 1024], P('grain', None, 'row'), may hold values from 0 to 0.5
- eigen_weight: float32 [64], P('grain'), may hold values from -1 to 1
- green: float32 [1024, 1024], replicated, may hold values from 0.25 to 2
Outputs:
- updated: float32 [64, 4, 1024, 1024], P('grain', None, 'row')
- potential: float32 [4, 1024, 1024], P(None, 'row')
The draws below stay inside these ranges and needn't reach their ends.
All inputs are finite; a program needn't handle non-finite values.
Results may differ from the reference program's by a relative error of at most 0.00016.
Values sent between devices are 32-bit elements; how exact they have to be, the bound alone decides.
A program may use at most 256 MiB of HBM per device.

```python
import math
import jax
import jax.numpy as jnp
from jax import lax

G = 64
N = 1024
PLANES = 4
STEPS = 3


def shard_levels(own_key, dims, shards, low, top_value):
    def one(position, parts):
        draws = jax.random.uniform(jax.random.fold_in(jax.random.fold_in(own_key, 6), position), (parts,), jnp.float32, low / len(shards), top_value / len(shards))
        return jnp.repeat(jnp.exp(draws), dims[position] // parts).reshape((-1,) + (1,) * (len(dims) - position - 1))

    factor_of = one(*shards[0])
    for cut in shards[1:]:
        factor_of = factor_of * one(*cut)
    return factor_of


def setup_inputs(seed: int = 0) -> dict:
    keys = jax.random.split(jax.random.key(seed), 4)
    order_params = jnp.clip(0.5 * jax.random.uniform(keys[0], (G, PLANES, N, N), jnp.float32) ** shard_levels(keys[0], (G, PLANES, N, N), ((0, 4), (2, 8)), -0.2, 0.2), 0.0, 0.5)
    eigen_weight = jnp.clip(jax.random.uniform(keys[1], (G,), jnp.float32, -1.0, 1.0) * shard_levels(keys[1], (G,), ((0, 4),), -0.4, 0.0), -1.0, 1.0)
    green = jnp.clip(jnp.exp(jax.random.uniform(keys[2], (N, N), jnp.float32, math.log(0.25), math.log(2.0))), 0.25, 2.0)
    return {"order_params": order_params, "eigen_weight": eigen_weight, "green": green}


time_step = 0.1
alpha_coef = 1.0
beta_coef = 1.0
gamma_coef = 0.25
kappa_coef = 1.0
elastic_coef = 2.0


def evolve_plane(plane):
    order = plane
    for repeat in range(STEPS):
        totals = jnp.sum(order * order, axis=0)
        laplacian = jnp.roll(order, 1, 1) + jnp.roll(order, -1, 1) + jnp.roll(order, 1, 2) + jnp.roll(order, -1, 2) - 4.0 * order
        others = totals[None] - order * order
        chemical = -alpha_coef * order + beta_coef * order ** 3 + 2.0 * gamma_coef * order * others - kappa_coef * laplacian
        order = order - time_step * chemical
    return order


def reference(order_params, eigen_weight, green):
    planes_first = jnp.moveaxis(order_params, 1, 0)
    evolved = lax.map(evolve_plane, planes_first)
    strain = jnp.sum(eigen_weight[None, :, None, None] * evolved * evolved, axis=1)
    spectrum = jnp.fft.fft2(strain, axes=(-2, -1))
    potential = jnp.real(jnp.fft.ifft2(green[None] * spectrum, axes=(-2, -1))).astype(strain.dtype)
    factor = time_step * 2.0 * elastic_coef
    updated = evolved - factor * eigen_weight[None, :, None, None] * evolved * potential[:, None]
    return jnp.moveaxis(updated, 0, 1), potential
```

```python
import functools
import math

import jax
import jax.numpy as jnp
import numpy as np
from jax import lax
from jax.experimental import pallas as pl
from jax.experimental.pallas import tpu as pltpu
from jax.sharding import PartitionSpec as P

STEPS = 3

time_step = 0.1
alpha_coef = 1.0
beta_coef = 1.0
gamma_coef = 0.25
kappa_coef = 1.0
elastic_coef = 2.0

MESH = pl.DeviceIdType.MESH
HIGH = lax.Precision.HIGH
STRIP = 8


def steps_kernel(
    sizes, weight, order_in, order_out, strain_out,
    field, sums, send_up, send_down, in_up, in_down,
    edge_top, edge_bottom, halo_top, halo_bottom, above,
    load_sem, store_sem, strain_sem,
    up_send, up_recv, down_send, down_recv,
    top_send, top_recv, bottom_send, bottom_recv,
):
    chain, ring, grains, planes, rows, width = sizes
    z, r = lax.axis_index("grain"), lax.axis_index("row")
    before, after = lax.rem(r + ring - 1, ring), lax.rem(r + 1, ring)
    has_lower, has_upper = z > 0, z < chain - 1
    lower, upper = z - 1, z + 1
    lag_up = jnp.minimum(z, planes - 1)
    lag_down = jnp.minimum(chain - 1 - z, planes - 1)
    strips = rows // STRIP
    last = (STEPS + 1) * planes

    def load(p):
        return pltpu.make_async_copy(
            order_in.at[:, p], field.at[:, p, pl.ds(0, rows)], load_sem.at[p]
        )

    def store(p):
        return pltpu.make_async_copy(
            field.at[:, p, pl.ds(0, rows)], order_out.at[:, p], store_sem.at[p]
        )

    def up_copy(p, par):
        return pltpu.make_async_remote_copy(
            send_up.at[p], in_up.at[par, p], up_send.at[p], up_recv.at[par, p],
            device_id=(upper, r), device_id_type=MESH,
        )

    def down_copy(p, par):
        return pltpu.make_async_remote_copy(
            send_down.at[p], in_down.at[par, p], down_send.at[p], down_recv.at[par, p],
            device_id=(lower, r), device_id_type=MESH,
        )

    def top_copy(p, par):
        return pltpu.make_async_remote_copy(
            edge_top.at[p], halo_bottom.at[par, p], top_send.at[p], bottom_recv.at[par, p],
            device_id=(z, before), device_id_type=MESH,
        )

    def bottom_copy(p, par):
        return pltpu.make_async_remote_copy(
            edge_bottom.at[p], halo_top.at[par, p], bottom_send.at[p], top_recv.at[par, p],
            device_id=(z, after), device_id_type=MESH,
        )

    for p in range(planes):
        load(p).start()

    barrier = pltpu.get_barrier_semaphore()
    pl.semaphore_signal(barrier, inc=1, device_id=(z, before), device_id_type=MESH)
    pl.semaphore_signal(barrier, inc=1, device_id=(z, after), device_id_type=MESH)

    @pl.when(has_lower)
    def _():
        pl.semaphore_signal(barrier, inc=1, device_id=(lower, r), device_id_type=MESH)

    @pl.when(has_upper)
    def _():
        pl.semaphore_signal(barrier, inc=1, device_id=(upper, r), device_id_type=MESH)

    @pl.when(jnp.logical_not(has_lower))
    def _():
        in_up[...] = jnp.zeros_like(in_up)

    @pl.when(jnp.logical_not(has_upper))
    def _():
        in_down[...] = jnp.zeros_like(in_down)

    pl.semaphore_wait(barrier, 2 + has_lower.astype(jnp.int32) + has_upper.astype(jnp.int32))

    def send_edges(p, par):
        for g in range(grains):
            edge_top[p, pl.ds(g, 1), :] = field[g, p, pl.ds(0, 1), :]
            edge_bottom[p, pl.ds(g, 1), :] = field[g, p, pl.ds(rows - 1, 1), :]
        top_copy(p, par).start()
        bottom_copy(p, par).start()

    def first(p):
        load(p).wait()

        def strip(i, carry):
            at = pl.ds(pl.multiple_of(i * STRIP, STRIP), STRIP)
            total = jnp.zeros((STRIP, width), jnp.float32)
            for g in range(grains):
                value = field[g, p, at, :]
                total = total + value * value
            sums[p, at, :] = total
            return carry

        lax.fori_loop(0, strips, strip, 0)
        send_edges(p, 0)

    def advance(t, p, step):
        par = lax.rem(step, 2)
        bottom_copy(p, par).wait_recv()
        top_copy(p, par).wait_recv()
        above[...] = halo_top[par, p]
        for g in range(grains):
            field[g, p, pl.ds(rows, 1), :] = halo_bottom[par, p, pl.ds(g, 1), :]
        final = step == STEPS - 1
        row_id = lax.broadcasted_iota(jnp.int32, (STRIP, width), 0)
        scale = time_step * gamma_coef * 2.0
        base = 1.0 + time_step * alpha_coef - 4.0 * time_step * kappa_coef
        cube = time_step * beta_coef - scale
        spread = time_step * kappa_coef

        def strip(i, carry):
            start = pl.multiple_of(i * STRIP, STRIP)
            at = pl.ds(start, STRIP)
            total = sums[p, at, :] + (in_up[par, p, at, :] + in_down[par, p, at, :])
            shared = base - scale * total
            result = jnp.zeros((STRIP, width), jnp.float32)
            for g in range(grains):
                value = field[g, p, at, :]
                up_row = jnp.broadcast_to(above[pl.ds(g, 1), :], (STRIP, width))
                down_row = jnp.broadcast_to(
                    field[g, p, pl.ds(start + STRIP, 1), :], (STRIP, width)
                )
                above[pl.ds(g, 1), :] = value[STRIP - 1 :, :]
                up = jnp.where(row_id == 0, up_row, pltpu.roll(value, 1, 0))
                down = jnp.where(row_id == STRIP - 1, down_row, pltpu.roll(value, STRIP - 1, 0))
                around = (up + down) + (pltpu.roll(value, 1, 1) + pltpu.roll(value, width - 1, 1))
                fresh = value * (shared - cube * (value * value)) + spread * around
                field[g, p, at, :] = fresh
                factor = jnp.where(final, weight[g], 1.0)
                result = result + factor * (fresh * fresh)
            sums[p, at, :] = result
            return carry

        lax.fori_loop(0, strips, strip, 0)

        @pl.when(jnp.logical_not(final))
        def _():
            top_copy(p, par).wait_send()
            bottom_copy(p, par).wait_send()
            send_edges(p, 1 - par)

        @pl.when(final)
        def _():
            store(p).start()

    def add_into(target, p, incoming, par):
        def strip(i, carry):
            at = pl.ds(pl.multiple_of(i * STRIP, STRIP), STRIP)
            target[p, at, :] = incoming[par, p, at, :] + sums[p, at, :]
            return carry

        lax.fori_loop(0, strips, strip, 0)

    def forward_up(t):
        p, level = lax.rem(t, planes), t // planes
        par = lax.rem(level, 2)

        @pl.when(has_lower)
        def _():
            up_copy(p, par).wait_recv()

        @pl.when(has_upper)
        def _():
            @pl.when(level > 0)
            def _():
                up_copy(p, par).wait_send()

            add_into(send_up, p, in_up, par)
            up_copy(p, par).start()

    def forward_down(t):
        p, level = lax.rem(t, planes), t // planes
        par = lax.rem(level, 2)

        @pl.when(has_upper)
        def _():
            down_copy(p, par).wait_recv()

        @pl.when(has_lower)
        def _():
            @pl.when(level > 0)
            def _():
                down_copy(p, par).wait_send()

            add_into(send_down, p, in_down, par)
            down_copy(p, par).start()

    def slot(t, carry):
        p = lax.rem(t, planes)

        @pl.when(t < planes)
        def _():
            first(p)

        @pl.when(jnp.logical_and(t >= planes, t < last))
        def _():
            advance(t, p, t // planes - 1)

        up_t, down_t = t - lag_up, t - lag_down

        @pl.when(jnp.logical_and(up_t >= 0, up_t < last))
        def _():
            forward_up(up_t)

        @pl.when(jnp.logical_and(down_t >= 0, down_t < last))
        def _():
            forward_down(down_t)

        return carry

    lax.fori_loop(0, last + planes - 1, slot, 0)

    par = STEPS % 2
    for p in range(planes):
        def strip(i, carry):
            at = pl.ds(pl.multiple_of(i * STRIP, STRIP), STRIP)
            sums[p, at, :] = sums[p, at, :] + (in_up[par, p, at, :] + in_down[par, p, at, :])
            return carry

        lax.fori_loop(0, strips, strip, 0)
    out = pltpu.make_async_copy(sums, strain_out, strain_sem)
    out.start()
    for p in range(planes):
        top_copy(p, 0).wait_send()
        bottom_copy(p, 0).wait_send()
        store(p).wait()

        @pl.when(has_upper)
        def _():
            up_copy(p, par).wait_send()

        @pl.when(has_lower)
        def _():
            down_copy(p, par).wait_send()
    out.wait()


def run_steps(order, weight):
    chain, ring = lax.axis_size("grain"), lax.axis_size("row")
    grains, planes, rows, width = order.shape
    f32 = jnp.float32
    dma = pltpu.SemaphoreType.DMA
    plane = (planes, rows, width)
    edges = (planes, grains, width)
    return pl.pallas_call(
        functools.partial(steps_kernel, (chain, ring, grains, planes, rows, width)),
        out_shape=(
            jax.ShapeDtypeStruct(order.shape, f32),
            jax.ShapeDtypeStruct(plane, f32),
        ),
        in_specs=[pl.BlockSpec(memory_space=pltpu.SMEM), pl.BlockSpec(memory_space=pl.ANY)],
        out_specs=(pl.BlockSpec(memory_space=pl.ANY), pl.BlockSpec(memory_space=pl.ANY)),
        scratch_shapes=[
            pltpu.VMEM((grains, planes, rows + STRIP, width), f32),
            pltpu.VMEM(plane, f32),
            pltpu.VMEM(plane, f32),
            pltpu.VMEM(plane, f32),
            pltpu.VMEM((2,) + plane, f32),
            pltpu.VMEM((2,) + plane, f32),
            pltpu.VMEM(edges, f32),
            pltpu.VMEM(edges, f32),
            pltpu.VMEM((2,) + edges, f32),
            pltpu.VMEM((2,) + edges, f32),
            pltpu.VMEM((grains, width), f32),
            dma((planes,)),
            dma((planes,)),
            dma,
            dma((planes,)),
            dma((2, planes)),
            dma((planes,)),
            dma((2, planes)),
            dma((planes,)),
            dma((2, planes)),
            dma((planes,)),
            dma((2, planes)),
        ],
        compiler_params=pltpu.CompilerParams(
            collective_id=0, has_side_effects=True, vmem_limit_bytes=58 * 1024 * 1024
        ),
        cost_estimate=pl.CostEstimate(
            flops=60 * order.size, bytes_accessed=8 * order.size, transcendentals=0
        ),
    )(weight, order)


def row_tables(length, shares, ring):
    half = length // 2
    block = half // (shares * ring)
    places = np.arange(length)
    angle = 2.0 * math.pi / length * (np.outer(places, np.arange(half)) % length)
    cosine, sine = np.cos(angle), np.sin(angle)
    alternate = 1.0 - 2.0 * (places % 2)
    forward = np.stack([cosine, -sine], axis=1)
    forward[:, 1, 0] = alternate
    backward = 2.0 * np.stack([cosine, -sine], axis=1)
    backward[:, 0, 0] = 1.0
    backward[:, 1, 0] = alternate
    backward /= float(length) * float(length)

    def by_owner(table):
        table = table.reshape(length, 2, shares, ring, block).transpose(0, 2, 3, 1, 4)
        return table.reshape(length, shares, ring * 2 * block).astype(np.float32)

    return by_owner(forward).transpose(1, 0, 2).copy(), by_owner(backward).transpose(1, 2, 0).copy()


def column_table(length):
    places = np.arange(length)
    angle = 2.0 * math.pi / length * (np.outer(places, places) % length)
    return np.concatenate([np.cos(angle), np.sin(angle)], axis=0).astype(np.float32)


def flip_rows(x):
    return jnp.concatenate([x[:1], x[1:][::-1]], axis=0)


def even_green(green, start, block):
    length = green.shape[1]
    here = lax.dynamic_slice_in_dim(green, start, block, 1)
    tail = lax.dynamic_slice_in_dim(green, length - start - block, block, 1)
    head = lax.dynamic_slice_in_dim(green, (length - start) % length, 1, 1)
    mirror = jnp.concatenate([head, tail[:, ::-1][:, : block - 1]], axis=1)
    middle = green[:, length // 2 : length // 2 + 1]
    return 0.5 * (here + flip_rows(mirror)), 0.5 * (middle + flip_rows(middle))


def dot(a, b, dims):
    return lax.dot_general(
        a, b, (dims, ((), ())), precision=HIGH, preferred_element_type=jnp.float32
    )


def local(order_params, eigen_weight, green):
    order, strain = run_steps(order_params, eigen_weight)
    planes, rows, length = strain.shape
    chain, ring = lax.axis_size("grain"), lax.axis_size("row")
    z, r = lax.axis_index("grain"), lax.axis_index("row")
    shares = max(1, chain // planes)
    held = max(1, planes // chain)
    half = length // 2
    block = half // (shares * ring)
    forward, backward = row_tables(length, shares, ring)
    columns = jnp.asarray(column_table(length))
    part = z % shares
    start = (part * ring + r) * block
    even, middle = even_green(green, start, block)

    mine = lax.dynamic_slice_in_dim(strain, z // shares * held, held, 0).reshape(held * rows, length)
    pick = lambda table: lax.dynamic_index_in_dim(jnp.asarray(table), part, 0, keepdims=False)
    spectrum = dot(mine, pick(forward), ((1,), (0,)))
    spectrum = spectrum.reshape(held * rows, ring, 2 * block).transpose(1, 0, 2)
    spectrum = lax.all_to_all(spectrum, "row", split_axis=0, concat_axis=0, tiled=True)
    spectrum = spectrum.reshape(ring, held, rows, 2 * block).transpose(0, 2, 1, 3)
    spectrum = spectrum.reshape(ring * rows, held * 2 * block)

    product = dot(columns, spectrum, ((1,), (0,))).reshape(2, length, held, 2, block)
    cos_re, cos_im = product[0, :, :, 0], product[0, :, :, 1]
    sin_re, sin_im = product[1, :, :, 0], product[1, :, :, 1]
    packed = (start + jnp.arange(block) == 0)[None, None, :]
    g, m = even[:, None, :], middle[:, None, :]
    real, imag = g * (cos_re + sin_im), g * (cos_im - sin_re)
    x1 = jnp.where(packed, g * cos_re, real)
    x2 = jnp.where(packed, g * sin_re, -imag)
    x3 = jnp.where(packed, m * cos_im, imag)
    x4 = jnp.where(packed, m * sin_im, real)
    scaled = jnp.stack([jnp.stack([x1, x3], axis=2), jnp.stack([x2, x4], axis=2)], axis=0)
    scaled = scaled.reshape(2 * length, held * 2 * block)
    mixed = dot(columns, scaled, ((0,), (0,)))

    mixed = mixed.reshape(ring, rows, held, 2 * block).transpose(0, 2, 1, 3)
    mixed = mixed.reshape(ring, held * rows, 2 * block)
    mixed = lax.all_to_all(mixed, "row", split_axis=0, concat_axis=0, tiled=True)
    mixed = mixed.transpose(1, 0, 2).reshape(held * rows, ring * 2 * block)
    piece = dot(mixed, pick(backward), ((1,), (0,)))
    potential = lax.all_gather(piece, "grain", axis=0, tiled=True)
    if shares > 1:
        potential = jnp.sum(potential.reshape(planes, shares, rows, length), axis=1)
    potential = potential.reshape(planes, rows, length)
    factor = time_step * 2.0 * elastic_coef
    updated = order - factor * eigen_weight[:, None, None, None] * order * potential[None]
    return (updated, potential)


def solution(mesh):
    return jax.shard_map(
        local,
        mesh=mesh,
        in_specs=(P("grain", None, "row", None), P("grain"), P()),
        out_specs=(P("grain", None, "row", None), P(None, "row", None)),
        check_vma=False,
    )
```

```python
import functools
import math

import jax
import jax.numpy as jnp
import numpy as np
from jax import lax
from jax.experimental import pallas as pl
from jax.experimental.pallas import tpu as pltpu
from jax.sharding import PartitionSpec as P

STEPS = 3

time_step = 0.1
alpha_coef = 1.0
beta_coef = 1.0
gamma_coef = 0.25
kappa_coef = 1.0
elastic_coef = 2.0

MESH = pl.DeviceIdType.MESH
HIGH = lax.Precision.HIGH
STRIP = 8
PIECES = 4
GATHERS = 2


def steps_kernel(
    sizes, weight, order_in, order_out, strain_out,
    field, sums, send_up, send_down, in_up, in_down,
    edge_top, edge_bottom, halo_top, halo_bottom, above,
    load_sem, store_sem, strain_sem,
    up_send, up_recv, down_send, down_recv,
    top_send, top_recv, bottom_send, bottom_recv,
):
    chain, ring, grains, planes, rows, width = sizes
    z, r = lax.axis_index("grain"), lax.axis_index("row")
    before, after = lax.rem(r + ring - 1, ring), lax.rem(r + 1, ring)
    has_lower, has_upper = z > 0, z < chain - 1
    lower, upper = z - 1, z + 1
    lag_up = jnp.minimum(z, planes - 1)
    lag_down = jnp.minimum(chain - 1 - z, planes - 1)
    strips = rows // STRIP
    last = (STEPS + 1) * planes
    part = rows // PIECES
    held, shares = max(1, planes // chain), max(1, chain // planes)

    def plane_of(t):
        i = lax.rem(t, planes)
        odd = lax.rem(i, 2)
        return (1 - odd) * (i // 2) + odd * (planes - 1 - i // 2)

    def owners(p):
        low = p // held * shares
        return low, low + shares - 1

    def load(p):
        return pltpu.make_async_copy(
            order_in.at[:, p], field.at[:, p, pl.ds(0, rows)], load_sem.at[p]
        )

    def store(p):
        return pltpu.make_async_copy(
            field.at[:, p, pl.ds(0, rows)], order_out.at[:, p], store_sem.at[p]
        )

    def up_copy(p, par, c):
        at = pl.ds(c * part, part)
        return pltpu.make_async_remote_copy(
            send_up.at[p, at], in_up.at[par, p, at], up_send.at[p, c], up_recv.at[par, p, c],
            device_id=(upper, r), device_id_type=MESH,
        )

    def down_copy(p, par, c):
        at = pl.ds(c * part, part)
        return pltpu.make_async_remote_copy(
            send_down.at[p, at], in_down.at[par, p, at], down_send.at[p, c], down_recv.at[par, p, c],
            device_id=(lower, r), device_id_type=MESH,
        )

    def top_copy(p, par):
        return pltpu.make_async_remote_copy(
            edge_top.at[p], halo_bottom.at[par, p], top_send.at[p], bottom_recv.at[par, p],
            device_id=(z, before), device_id_type=MESH,
        )

    def bottom_copy(p, par):
        return pltpu.make_async_remote_copy(
            edge_bottom.at[p], halo_top.at[par, p], bottom_send.at[p], top_recv.at[par, p],
            device_id=(z, after), device_id_type=MESH,
        )

    for i in range(planes):
        load(plane_of(i)).start()

    barrier = pltpu.get_barrier_semaphore()
    pl.semaphore_signal(barrier, inc=1, device_id=(z, before), device_id_type=MESH)
    pl.semaphore_signal(barrier, inc=1, device_id=(z, after), device_id_type=MESH)

    @pl.when(has_lower)
    def _():
        pl.semaphore_signal(barrier, inc=1, device_id=(lower, r), device_id_type=MESH)

    @pl.when(has_upper)
    def _():
        pl.semaphore_signal(barrier, inc=1, device_id=(upper, r), device_id_type=MESH)

    @pl.when(jnp.logical_not(has_lower))
    def _():
        in_up[...] = jnp.zeros_like(in_up)

    @pl.when(jnp.logical_not(has_upper))
    def _():
        in_down[...] = jnp.zeros_like(in_down)

    pl.semaphore_wait(barrier, 2 + has_lower.astype(jnp.int32) + has_upper.astype(jnp.int32))

    def send_edges(p, par):
        for g in range(grains):
            edge_top[p, pl.ds(g, 1), :] = field[g, p, pl.ds(0, 1), :]
            edge_bottom[p, pl.ds(g, 1), :] = field[g, p, pl.ds(rows - 1, 1), :]
        top_copy(p, par).start()
        bottom_copy(p, par).start()

    def first(p):
        load(p).wait()

        def strip(i, carry):
            at = pl.ds(pl.multiple_of(i * STRIP, STRIP), STRIP)
            total = jnp.zeros((STRIP, width), jnp.float32)
            for g in range(grains):
                value = field[g, p, at, :]
                total = total + value * value
            sums[p, at, :] = total
            return carry

        lax.fori_loop(0, strips, strip, 0)
        send_edges(p, 0)

    def advance(t, p, step):
        par = lax.rem(step, 2)
        bottom_copy(p, par).wait_recv()
        top_copy(p, par).wait_recv()
        above[...] = halo_top[par, p]
        for g in range(grains):
            field[g, p, pl.ds(rows, 1), :] = halo_bottom[par, p, pl.ds(g, 1), :]
        final = step == STEPS - 1
        row_id = lax.broadcasted_iota(jnp.int32, (STRIP, width), 0)
        scale = time_step * gamma_coef * 2.0
        base = 1.0 + time_step * alpha_coef - 4.0 * time_step * kappa_coef
        cube = time_step * beta_coef - scale
        spread = time_step * kappa_coef

        def strip(i, carry):
            start = pl.multiple_of(i * STRIP, STRIP)
            at = pl.ds(start, STRIP)
            total = sums[p, at, :] + (in_up[par, p, at, :] + in_down[par, p, at, :])
            shared = base - scale * total
            result = jnp.zeros((STRIP, width), jnp.float32)
            for g in range(grains):
                value = field[g, p, at, :]
                up_row = jnp.broadcast_to(above[pl.ds(g, 1), :], (STRIP, width))
                down_row = jnp.broadcast_to(
                    field[g, p, pl.ds(start + STRIP, 1), :], (STRIP, width)
                )
                above[pl.ds(g, 1), :] = value[STRIP - 1 :, :]
                up = jnp.where(row_id == 0, up_row, pltpu.roll(value, 1, 0))
                down = jnp.where(row_id == STRIP - 1, down_row, pltpu.roll(value, STRIP - 1, 0))
                around = (up + down) + (pltpu.roll(value, 1, 1) + pltpu.roll(value, width - 1, 1))
                fresh = value * (shared - cube * (value * value)) + spread * around
                field[g, p, at, :] = fresh
                factor = jnp.where(final, weight[g], 1.0)
                result = result + factor * (fresh * fresh)
            sums[p, at, :] = result
            return carry

        lax.fori_loop(0, strips, strip, 0)

        @pl.when(jnp.logical_not(final))
        def _():
            top_copy(p, par).wait_send()
            bottom_copy(p, par).wait_send()
            send_edges(p, 1 - par)

        @pl.when(final)
        def _():
            store(p).start()

    def add_into(target, p, incoming, par, c):
        def strip(i, carry):
            at = pl.ds(pl.multiple_of(c * part + i * STRIP, STRIP), STRIP)
            target[p, at, :] = incoming[par, p, at, :] + sums[p, at, :]
            return carry

        lax.fori_loop(0, part // STRIP, strip, 0)

    def forward(t, copy, incoming, target, takes, gives):
        p, level = plane_of(t), t // planes
        par = lax.rem(level, 2)
        for c in range(PIECES):
            @pl.when(takes(p, level))
            def _():
                copy(p, par, c).wait_recv()

            @pl.when(gives(p, level))
            def _():
                @pl.when(level > 0)
                def _():
                    copy(p, par, c).wait_send()

                add_into(target, p, incoming, par, c)
                copy(p, par, c).start()

    def takes_up(p, level):
        return jnp.logical_and(has_lower, jnp.logical_or(level < STEPS, z <= owners(p)[1]))

    def gives_up(p, level):
        return jnp.logical_and(has_upper, jnp.logical_or(level < STEPS, z < owners(p)[1]))

    def takes_down(p, level):
        return jnp.logical_and(has_upper, jnp.logical_or(level < STEPS, z >= owners(p)[0]))

    def gives_down(p, level):
        return jnp.logical_and(has_lower, jnp.logical_or(level < STEPS, z > owners(p)[0]))

    def forward_up(t):
        forward(t, up_copy, in_up, send_up, takes_up, gives_up)

    def forward_down(t):
        forward(t, down_copy, in_down, send_down, takes_down, gives_down)

    def slot(t, carry):
        p = plane_of(t)

        @pl.when(t < planes)
        def _():
            first(p)

        @pl.when(jnp.logical_and(t >= planes, t < last))
        def _():
            advance(t, p, t // planes - 1)

        up_t, down_t = t - lag_up, t - lag_down

        @pl.when(jnp.logical_and(up_t >= 0, up_t < last))
        def _():
            forward_up(up_t)

        @pl.when(jnp.logical_and(down_t >= 0, down_t < last))
        def _():
            forward_down(down_t)

        return carry

    lax.fori_loop(0, last + planes - 1, slot, 0)

    par = STEPS % 2
    mine = z // shares * held
    for k in range(held):
        def strip(i, carry):
            at = pl.ds(pl.multiple_of(i * STRIP, STRIP), STRIP)
            p = mine + k
            sums[p, at, :] = sums[p, at, :] + (in_up[par, p, at, :] + in_down[par, p, at, :])
            return carry

        lax.fori_loop(0, strips, strip, 0)
    out = pltpu.make_async_copy(sums.at[pl.ds(mine, held)], strain_out, strain_sem)
    out.start()
    for p in range(planes):
        top_copy(p, 0).wait_send()
        bottom_copy(p, 0).wait_send()
        store(p).wait()
        for c in range(PIECES):
            @pl.when(has_upper)
            def _():
                up_copy(p, par, c).wait_send()

            @pl.when(has_lower)
            def _():
                down_copy(p, par, c).wait_send()
    out.wait()


def run_steps(order, weight):
    chain, ring = lax.axis_size("grain"), lax.axis_size("row")
    grains, planes, rows, width = order.shape
    f32 = jnp.float32
    dma = pltpu.SemaphoreType.DMA
    plane = (planes, rows, width)
    edges = (planes, grains, width)
    return pl.pallas_call(
        functools.partial(steps_kernel, (chain, ring, grains, planes, rows, width)),
        out_shape=(
            jax.ShapeDtypeStruct(order.shape, f32),
            jax.ShapeDtypeStruct((max(1, planes // chain), rows, width), f32),
        ),
        in_specs=[pl.BlockSpec(memory_space=pltpu.SMEM), pl.BlockSpec(memory_space=pl.ANY)],
        out_specs=(pl.BlockSpec(memory_space=pl.ANY), pl.BlockSpec(memory_space=pl.ANY)),
        scratch_shapes=[
            pltpu.VMEM((grains, planes, rows + STRIP, width), f32),
            pltpu.VMEM(plane, f32),
            pltpu.VMEM(plane, f32),
            pltpu.VMEM(plane, f32),
            pltpu.VMEM((2,) + plane, f32),
            pltpu.VMEM((2,) + plane, f32),
            pltpu.VMEM(edges, f32),
            pltpu.VMEM(edges, f32),
            pltpu.VMEM((2,) + edges, f32),
            pltpu.VMEM((2,) + edges, f32),
            pltpu.VMEM((grains, width), f32),
            dma((planes,)),
            dma((planes,)),
            dma,
            dma((planes, PIECES)),
            dma((2, planes, PIECES)),
            dma((planes, PIECES)),
            dma((2, planes, PIECES)),
            dma((planes,)),
            dma((2, planes)),
            dma((planes,)),
            dma((2, planes)),
        ],
        compiler_params=pltpu.CompilerParams(
            collective_id=0, has_side_effects=True, vmem_limit_bytes=58 * 1024 * 1024
        ),
        cost_estimate=pl.CostEstimate(
            flops=60 * order.size, bytes_accessed=8 * order.size, transcendentals=0
        ),
    )(weight, order)


def row_tables(length, shares, ring):
    half = length // 2
    block = half // (shares * ring)
    places = np.arange(length)
    angle = 2.0 * math.pi / length * (np.outer(places, np.arange(half)) % length)
    cosine, sine = np.cos(angle), np.sin(angle)
    alternate = 1.0 - 2.0 * (places % 2)
    forward = np.stack([cosine, -sine], axis=1)
    forward[:, 1, 0] = alternate
    backward = 2.0 * np.stack([cosine, -sine], axis=1)
    backward[:, 0, 0] = 1.0
    backward[:, 1, 0] = alternate
    backward /= float(length) * float(length)

    def by_owner(table):
        table = table.reshape(length, 2, shares, ring, block).transpose(0, 2, 3, 1, 4)
        return table.reshape(length, shares, ring * 2 * block).astype(np.float32)

    return by_owner(forward).transpose(1, 0, 2).copy(), by_owner(backward).transpose(1, 2, 0).copy()


def column_table(length):
    places = np.arange(length)
    angle = 2.0 * math.pi / length * (np.outer(places, places) % length)
    return np.concatenate([np.cos(angle), np.sin(angle)], axis=0).astype(np.float32)


def flip_rows(x):
    return jnp.concatenate([x[:1], x[1:][::-1]], axis=0)


def even_green(green, start, block):
    length = green.shape[1]
    here = lax.dynamic_slice_in_dim(green, start, block, 1)
    tail = lax.dynamic_slice_in_dim(green, length - start - block, block, 1)
    head = lax.dynamic_slice_in_dim(green, (length - start) % length, 1, 1)
    mirror = jnp.concatenate([head, tail[:, ::-1][:, : block - 1]], axis=1)
    middle = green[:, length // 2 : length // 2 + 1]
    return 0.5 * (here + flip_rows(mirror)), 0.5 * (middle + flip_rows(middle))


def dot(a, b, dims):
    return lax.dot_general(
        a, b, (dims, ((), ())), precision=HIGH, preferred_element_type=jnp.float32
    )


def update_kernel(grains, weight, order, potential, *rest):
    out = rest[-1]
    factor = time_step * 2.0 * elastic_coef
    for i in range(grains):
        scale = factor * weight[pl.program_id(0) * grains + i]
        value = order[i]
        out[i] = value - scale * value * potential[...]


def update_rows(k, weight, order, potential, filled):
    grains, planes, rows, width = order.shape
    part = potential.shape[1]
    group = math.gcd(grains, 2)
    block = pl.BlockSpec((group, planes, part, width), lambda g: (g, 0, k, 0))
    whole = pl.BlockSpec((planes, part, width), lambda g: (0, 0, 0))
    extra = [] if filled is None else [filled]
    return pl.pallas_call(
        functools.partial(update_kernel, group),
        grid=(grains // group,),
        out_shape=jax.ShapeDtypeStruct(order.shape, order.dtype),
        in_specs=[pl.BlockSpec(memory_space=pltpu.SMEM), block, whole]
        + [pl.BlockSpec(memory_space=pl.ANY)] * len(extra),
        out_specs=block,
        input_output_aliases={3: 0} if extra else {},
        cost_estimate=pl.CostEstimate(
            flops=3 * order.size * part // rows,
            bytes_accessed=8 * order.size * part // rows,
            transcendentals=0,
        ),
        compiler_params=pltpu.CompilerParams(vmem_limit_bytes=32 * 1024 * 1024),
    )(weight, order, potential, *extra)


def local(order_params, eigen_weight, green):
    order, strain = run_steps(order_params, eigen_weight)
    planes = order.shape[1]
    held, rows, length = strain.shape
    chain, ring = lax.axis_size("grain"), lax.axis_size("row")
    z, r = lax.axis_index("grain"), lax.axis_index("row")
    shares = max(1, chain // planes)
    half = length // 2
    block = half // (shares * ring)
    forward, backward = row_tables(length, shares, ring)
    columns = jnp.asarray(column_table(length))
    part = z % shares
    start = (part * ring + r) * block
    even, middle = even_green(green, start, block)

    mine = strain.reshape(held * rows, length)
    pick = lambda table: lax.dynamic_index_in_dim(jnp.asarray(table), part, 0, keepdims=False)
    spectrum = dot(mine, pick(forward), ((1,), (0,)))
    spectrum = spectrum.reshape(held * rows, ring, 2 * block).transpose(1, 0, 2)
    spectrum = lax.all_to_all(spectrum, "row", split_axis=0, concat_axis=0, tiled=True)
    spectrum = spectrum.reshape(ring, held, rows, 2 * block).transpose(0, 2, 1, 3)
    spectrum = spectrum.reshape(ring * rows, held * 2 * block)

    product = dot(columns, spectrum, ((1,), (0,))).reshape(2, length, held, 2, block)
    cos_re, cos_im = product[0, :, :, 0], product[0, :, :, 1]
    sin_re, sin_im = product[1, :, :, 0], product[1, :, :, 1]
    packed = (start + jnp.arange(block) == 0)[None, None, :]
    g, m = even[:, None, :], middle[:, None, :]
    real, imag = g * (cos_re + sin_im), g * (cos_im - sin_re)
    x1 = jnp.where(packed, g * cos_re, real)
    x2 = jnp.where(packed, g * sin_re, -imag)
    x3 = jnp.where(packed, m * cos_im, imag)
    x4 = jnp.where(packed, m * sin_im, real)
    scaled = jnp.stack([jnp.stack([x1, x3], axis=2), jnp.stack([x2, x4], axis=2)], axis=0)
    scaled = scaled.reshape(2 * length, held * 2 * block)
    mixed = dot(columns, scaled, ((0,), (0,)))

    mixed = mixed.reshape(ring, rows, held, 2 * block).transpose(0, 2, 1, 3)
    mixed = mixed.reshape(ring, held * rows, 2 * block)
    mixed = lax.all_to_all(mixed, "row", split_axis=0, concat_axis=0, tiled=True)
    mixed = mixed.transpose(1, 0, 2).reshape(held * rows, ring * 2 * block)
    piece = dot(mixed, pick(backward), ((1,), (0,)))
    piece = piece.reshape(held, rows, length)
    updated, gathered = None, []
    part = rows // GATHERS
    for k in range(GATHERS):
        potential = lax.all_gather(
            piece[:, k * part : (k + 1) * part], "grain", axis=0, tiled=True
        )
        if shares > 1:
            potential = jnp.sum(potential.reshape(planes, shares, part, length), axis=1)
        gathered.append(potential)
        updated = update_rows(k, eigen_weight, order, potential, updated)
    return (updated, jnp.concatenate(gathered, axis=1))


def solution(mesh):
    return jax.shard_map(
        local,
        mesh=mesh,
        in_specs=(P("grain", None, "row", None), P("grain"), P()),
        out_specs=(P("grain", None, "row", None), P(None, "row", None)),
        check_vma=False,
    )
```

```python
import functools
import math

import jax
import jax.numpy as jnp
import numpy as np
from jax import lax
from jax.experimental import pallas as pl
from jax.experimental.pallas import tpu as pltpu
from jax.sharding import PartitionSpec as P

STEPS = 3

time_step = 0.1
alpha_coef = 1.0
beta_coef = 1.0
gamma_coef = 0.25
kappa_coef = 1.0
elastic_coef = 2.0

MESH = pl.DeviceIdType.MESH
HIGH = lax.Precision.HIGH
STRIP = 8
PIECES = 4


def steps_kernel(
    sizes, weight, order_in, order_out, strain_out,
    field, sums, send_up, send_down, in_up, in_down,
    edge_top, edge_bottom, halo_top, halo_bottom, above,
    load_sem, store_sem, strain_sem,
    up_send, up_recv, down_send, down_recv,
    top_send, top_recv, bottom_send, bottom_recv,
):
    chain, ring, grains, planes, rows, width = sizes
    z, r = lax.axis_index("grain"), lax.axis_index("row")
    before, after = lax.rem(r + ring - 1, ring), lax.rem(r + 1, ring)
    has_lower, has_upper = z > 0, z < chain - 1
    lower, upper = z - 1, z + 1
    lag_up = jnp.minimum(z, planes - 1)
    lag_down = jnp.minimum(chain - 1 - z, planes - 1)
    strips = rows // STRIP
    last = (STEPS + 1) * planes
    part = rows // PIECES
    held, shares = max(1, planes // chain), max(1, chain // planes)

    def plane_of(t):
        i = lax.rem(t, planes)
        odd = lax.rem(i, 2)
        return (1 - odd) * (i // 2) + odd * (planes - 1 - i // 2)

    def owners(p):
        low = p // held * shares
        return low, low + shares - 1

    def load(p):
        return pltpu.make_async_copy(
            order_in.at[:, p], field.at[:, p, pl.ds(0, rows)], load_sem.at[p]
        )

    def store(p):
        return pltpu.make_async_copy(
            field.at[:, p, pl.ds(0, rows)], order_out.at[:, p], store_sem.at[p]
        )

    def up_copy(p, par, c):
        at = pl.ds(c * part, part)
        return pltpu.make_async_remote_copy(
            send_up.at[p, at], in_up.at[par, p, at], up_send.at[p, c], up_recv.at[par, p, c],
            device_id=(upper, r), device_id_type=MESH,
        )

    def down_copy(p, par, c):
        at = pl.ds(c * part, part)
        return pltpu.make_async_remote_copy(
            send_down.at[p, at], in_down.at[par, p, at], down_send.at[p, c], down_recv.at[par, p, c],
            device_id=(lower, r), device_id_type=MESH,
        )

    def top_copy(p, par):
        return pltpu.make_async_remote_copy(
            edge_top.at[p], halo_bottom.at[par, p], top_send.at[p], bottom_recv.at[par, p],
            device_id=(z, before), device_id_type=MESH,
        )

    def bottom_copy(p, par):
        return pltpu.make_async_remote_copy(
            edge_bottom.at[p], halo_top.at[par, p], bottom_send.at[p], top_recv.at[par, p],
            device_id=(z, after), device_id_type=MESH,
        )

    for i in range(planes):
        load(plane_of(i)).start()

    barrier = pltpu.get_barrier_semaphore()
    pl.semaphore_signal(barrier, inc=1, device_id=(z, before), device_id_type=MESH)
    pl.semaphore_signal(barrier, inc=1, device_id=(z, after), device_id_type=MESH)

    @pl.when(has_lower)
    def _():
        pl.semaphore_signal(barrier, inc=1, device_id=(lower, r), device_id_type=MESH)

    @pl.when(has_upper)
    def _():
        pl.semaphore_signal(barrier, inc=1, device_id=(upper, r), device_id_type=MESH)

    @pl.when(jnp.logical_not(has_lower))
    def _():
        in_up[...] = jnp.zeros_like(in_up)

    @pl.when(jnp.logical_not(has_upper))
    def _():
        in_down[...] = jnp.zeros_like(in_down)

    pl.semaphore_wait(barrier, 2 + has_lower.astype(jnp.int32) + has_upper.astype(jnp.int32))

    def send_edges(p, par):
        for g in range(grains):
            edge_top[p, pl.ds(g, 1), :] = field[g, p, pl.ds(0, 1), :]
            edge_bottom[p, pl.ds(g, 1), :] = field[g, p, pl.ds(rows - 1, 1), :]
        top_copy(p, par).start()
        bottom_copy(p, par).start()

    def first(p):
        load(p).wait()

        def strip(i, carry):
            at = pl.ds(pl.multiple_of(i * STRIP, STRIP), STRIP)
            total = jnp.zeros((STRIP, width), jnp.float32)
            for g in range(grains):
                value = field[g, p, at, :]
                total = total + value * value
            sums[p, at, :] = total
            return carry

        lax.fori_loop(0, strips, strip, 0)
        send_edges(p, 0)

    def advance(t, p, step):
        par = lax.rem(step, 2)
        bottom_copy(p, par).wait_recv()
        top_copy(p, par).wait_recv()
        above[...] = halo_top[par, p]
        for g in range(grains):
            field[g, p, pl.ds(rows, 1), :] = halo_bottom[par, p, pl.ds(g, 1), :]
        final = step == STEPS - 1
        row_id = lax.broadcasted_iota(jnp.int32, (STRIP, width), 0)
        scale = time_step * gamma_coef * 2.0
        base = 1.0 + time_step * alpha_coef - 4.0 * time_step * kappa_coef
        cube = time_step * beta_coef - scale
        spread = time_step * kappa_coef

        def strip(i, carry):
            start = pl.multiple_of(i * STRIP, STRIP)
            at = pl.ds(start, STRIP)
            total = sums[p, at, :] + (in_up[par, p, at, :] + in_down[par, p, at, :])
            shared = base - scale * total
            result = jnp.zeros((STRIP, width), jnp.float32)
            for g in range(grains):
                value = field[g, p, at, :]
                up_row = jnp.broadcast_to(above[pl.ds(g, 1), :], (STRIP, width))
                down_row = jnp.broadcast_to(
                    field[g, p, pl.ds(start + STRIP, 1), :], (STRIP, width)
                )
                above[pl.ds(g, 1), :] = value[STRIP - 1 :, :]
                up = jnp.where(row_id == 0, up_row, pltpu.roll(value, 1, 0))
                down = jnp.where(row_id == STRIP - 1, down_row, pltpu.roll(value, STRIP - 1, 0))
                around = (up + down) + (pltpu.roll(value, 1, 1) + pltpu.roll(value, width - 1, 1))
                fresh = value * (shared - cube * (value * value)) + spread * around
                field[g, p, at, :] = fresh
                factor = jnp.where(final, weight[g], 1.0)
                result = result + factor * (fresh * fresh)
            sums[p, at, :] = result
            return carry

        lax.fori_loop(0, strips, strip, 0)

        @pl.when(jnp.logical_not(final))
        def _():
            top_copy(p, par).wait_send()
            bottom_copy(p, par).wait_send()
            send_edges(p, 1 - par)

        @pl.when(final)
        def _():
            store(p).start()

    def add_into(target, p, incoming, par, c):
        def strip(i, carry):
            at = pl.ds(pl.multiple_of(c * part + i * STRIP, STRIP), STRIP)
            target[p, at, :] = incoming[par, p, at, :] + sums[p, at, :]
            return carry

        lax.fori_loop(0, part // STRIP, strip, 0)

    def forward(t, copy, incoming, target, takes, gives):
        p, level = plane_of(t), t // planes
        par = lax.rem(level, 2)
        for c in range(PIECES):
            @pl.when(takes(p, level))
            def _():
                copy(p, par, c).wait_recv()

            @pl.when(gives(p, level))
            def _():
                @pl.when(level > 0)
                def _():
                    copy(p, par, c).wait_send()

                add_into(target, p, incoming, par, c)
                copy(p, par, c).start()

    def takes_up(p, level):
        return jnp.logical_and(has_lower, jnp.logical_or(level < STEPS, z <= owners(p)[1]))

    def gives_up(p, level):
        return jnp.logical_and(has_upper, jnp.logical_or(level < STEPS, z < owners(p)[1]))

    def takes_down(p, level):
        return jnp.logical_and(has_upper, jnp.logical_or(level < STEPS, z >= owners(p)[0]))

    def gives_down(p, level):
        return jnp.logical_and(has_lower, jnp.logical_or(level < STEPS, z > owners(p)[0]))

    def forward_up(t):
        forward(t, up_copy, in_up, send_up, takes_up, gives_up)

    def forward_down(t):
        forward(t, down_copy, in_down, send_down, takes_down, gives_down)

    def slot(t, carry):
        p = plane_of(t)

        @pl.when(t < planes)
        def _():
            first(p)

        @pl.when(jnp.logical_and(t >= planes, t < last))
        def _():
            advance(t, p, t // planes - 1)

        up_t, down_t = t - lag_up, t - lag_down

        @pl.when(jnp.logical_and(up_t >= 0, up_t < last))
        def _():
            forward_up(up_t)

        @pl.when(jnp.logical_and(down_t >= 0, down_t < last))
        def _():
            forward_down(down_t)

        return carry

    lax.fori_loop(0, last + planes - 1, slot, 0)

    par = STEPS % 2
    mine = z // shares * held
    for k in range(held):
        def strip(i, carry):
            at = pl.ds(pl.multiple_of(i * STRIP, STRIP), STRIP)
            p = mine + k
            sums[p, at, :] = sums[p, at, :] + (in_up[par, p, at, :] + in_down[par, p, at, :])
            return carry

        lax.fori_loop(0, strips, strip, 0)
    out = pltpu.make_async_copy(sums.at[pl.ds(mine, held)], strain_out, strain_sem)
    out.start()
    for p in range(planes):
        top_copy(p, 0).wait_send()
        bottom_copy(p, 0).wait_send()
        store(p).wait()
        for c in range(PIECES):
            @pl.when(has_upper)
            def _():
                up_copy(p, par, c).wait_send()

            @pl.when(has_lower)
            def _():
                down_copy(p, par, c).wait_send()
    out.wait()


def run_steps(order, weight):
    chain, ring = lax.axis_size("grain"), lax.axis_size("row")
    grains, planes, rows, width = order.shape
    f32 = jnp.float32
    dma = pltpu.SemaphoreType.DMA
    plane = (planes, rows, width)
    edges = (planes, grains, width)
    return pl.pallas_call(
        functools.partial(steps_kernel, (chain, ring, grains, planes, rows, width)),
        out_shape=(
            jax.ShapeDtypeStruct(order.shape, f32),
            jax.ShapeDtypeStruct((max(1, planes // chain), rows, width), f32),
        ),
        in_specs=[pl.BlockSpec(memory_space=pltpu.SMEM), pl.BlockSpec(memory_space=pl.ANY)],
        out_specs=(pl.BlockSpec(memory_space=pl.ANY), pl.BlockSpec(memory_space=pl.ANY)),
        scratch_shapes=[
            pltpu.VMEM((grains, planes, rows + STRIP, width), f32),
            pltpu.VMEM(plane, f32),
            pltpu.VMEM(plane, f32),
            pltpu.VMEM(plane, f32),
            pltpu.VMEM((2,) + plane, f32),
            pltpu.VMEM((2,) + plane, f32),
            pltpu.VMEM(edges, f32),
            pltpu.VMEM(edges, f32),
            pltpu.VMEM((2,) + edges, f32),
            pltpu.VMEM((2,) + edges, f32),
            pltpu.VMEM((grains, width), f32),
            dma((planes,)),
            dma((planes,)),
            dma,
            dma((planes, PIECES)),
            dma((2, planes, PIECES)),
            dma((planes, PIECES)),
            dma((2, planes, PIECES)),
            dma((planes,)),
            dma((2, planes)),
            dma((planes,)),
            dma((2, planes)),
        ],
        compiler_params=pltpu.CompilerParams(
            collective_id=0, has_side_effects=True, vmem_limit_bytes=58 * 1024 * 1024
        ),
        cost_estimate=pl.CostEstimate(
            flops=60 * order.size, bytes_accessed=8 * order.size, transcendentals=0
        ),
    )(weight, order)


def row_tables(length, shares, ring):
    half = length // 2
    block = half // (shares * ring)
    places = np.arange(length)
    angle = 2.0 * math.pi / length * (np.outer(places, np.arange(half)) % length)
    cosine, sine = np.cos(angle), np.sin(angle)
    alternate = 1.0 - 2.0 * (places % 2)
    forward = np.stack([cosine, -sine], axis=1)
    forward[:, 1, 0] = alternate
    backward = 2.0 * np.stack([cosine, -sine], axis=1)
    backward[:, 0, 0] = 1.0
    backward[:, 1, 0] = alternate
    backward /= float(length) * float(length)

    def by_owner(table):
        table = table.reshape(length, 2, shares, ring, block).transpose(0, 2, 3, 1, 4)
        return table.reshape(length, shares, ring * 2 * block).astype(np.float32)

    return by_owner(forward).transpose(1, 0, 2).copy(), by_owner(backward).transpose(1, 2, 0).copy()


def column_table(length):
    places = np.arange(length)
    angle = 2.0 * math.pi / length * (np.outer(places, places) % length)
    return np.concatenate([np.cos(angle), np.sin(angle)], axis=0).astype(np.float32)


def flip_rows(x):
    return jnp.concatenate([x[:1], x[1:][::-1]], axis=0)


def even_green(green, start, block):
    length = green.shape[1]
    here = lax.dynamic_slice_in_dim(green, start, block, 1)
    tail = lax.dynamic_slice_in_dim(green, length - start - block, block, 1)
    head = lax.dynamic_slice_in_dim(green, (length - start) % length, 1, 1)
    mirror = jnp.concatenate([head, tail[:, ::-1][:, : block - 1]], axis=1)
    middle = green[:, length // 2 : length // 2 + 1]
    return 0.5 * (here + flip_rows(mirror)), 0.5 * (middle + flip_rows(middle))


def dot(a, b, dims):
    return lax.dot_general(
        a, b, (dims, ((), ())), precision=HIGH, preferred_element_type=jnp.float32
    )


def local(order_params, eigen_weight, green):
    order, strain = run_steps(order_params, eigen_weight)
    planes = order.shape[1]
    held, rows, length = strain.shape
    chain, ring = lax.axis_size("grain"), lax.axis_size("row")
    z, r = lax.axis_index("grain"), lax.axis_index("row")
    shares = max(1, chain // planes)
    half = length // 2
    block = half // (shares * ring)
    forward, backward = row_tables(length, shares, ring)
    columns = jnp.asarray(column_table(length))
    part = z % shares
    start = (part * ring + r) * block
    even, middle = even_green(green, start, block)

    mine = strain.reshape(held * rows, length)
    pick = lambda table: lax.dynamic_index_in_dim(jnp.asarray(table), part, 0, keepdims=False)
    spectrum = dot(mine, pick(forward), ((1,), (0,)))
    spectrum = spectrum.reshape(held * rows, ring, 2 * block).transpose(1, 0, 2)
    spectrum = lax.all_to_all(spectrum, "row", split_axis=0, concat_axis=0, tiled=True)
    spectrum = spectrum.reshape(ring, held, rows, 2 * block).transpose(0, 2, 1, 3)
    spectrum = spectrum.reshape(ring * rows, held * 2 * block)

    product = dot(columns, spectrum, ((1,), (0,))).reshape(2, length, held, 2, block)
    cos_re, cos_im = product[0, :, :, 0], product[0, :, :, 1]
    sin_re, sin_im = product[1, :, :, 0], product[1, :, :, 1]
    packed = (start + jnp.arange(block) == 0)[None, None, :]
    g, m = even[:, None, :], middle[:, None, :]
    real, imag = g * (cos_re + sin_im), g * (cos_im - sin_re)
    x1 = jnp.where(packed, g * cos_re, real)
    x2 = jnp.where(packed, g * sin_re, -imag)
    x3 = jnp.where(packed, m * cos_im, imag)
    x4 = jnp.where(packed, m * sin_im, real)
    scaled = jnp.stack([jnp.stack([x1, x3], axis=2), jnp.stack([x2, x4], axis=2)], axis=0)
    scaled = scaled.reshape(2 * length, held * 2 * block)
    mixed = dot(columns, scaled, ((0,), (0,)))

    mixed = mixed.reshape(ring, rows, held, 2 * block).transpose(0, 2, 1, 3)
    mixed = mixed.reshape(ring, held * rows, 2 * block)
    mixed = lax.all_to_all(mixed, "row", split_axis=0, concat_axis=0, tiled=True)
    mixed = mixed.transpose(1, 0, 2).reshape(held * rows, ring * 2 * block)
    piece = dot(mixed, pick(backward), ((1,), (0,)))
    potential = lax.all_gather(piece, "grain", axis=0, tiled=True)
    if shares > 1:
        potential = jnp.sum(potential.reshape(planes, shares, rows, length), axis=1)
    potential = potential.reshape(planes, rows, length)
    factor = time_step * 2.0 * elastic_coef
    updated = order - factor * eigen_weight[:, None, None, None] * order * potential[None]
    return (updated, potential)


def solution(mesh):
    return jax.shard_map(
        local,
        mesh=mesh,
        in_specs=(P("grain", None, "row", None), P("grain"), P()),
        out_specs=(P("grain", None, "row", None), P(None, "row", None)),
        check_vma=False,
    )
```
